512 devices in a mesh: store: 32 (over x, y), seq: 16 (over z, core).
Axes of the slice: x: 4, y: 8, z: 8, core: 2. Of those that a mesh axis runs over, the one named last changes fastest.
Arguments:
- store_pages: bfloat16 [128, 64, 2048], P('store'), may hold values from -6 to 6
- page_home: int32 [128], replicated, may hold values from 0 to 127, as said below
- doc_page: int32 [32, 3, 8], replicated, may hold values from 0 to 127, as said below
- prefix_len: int32 [32, 3], replicated, may hold values from 1 to 512, as said below
- suffix_q: bfloat16 [32, 1024, 12288], P('store', 'seq'), may hold values from -140 to 140
- suffix_kv: bfloat16 [32, 1024, 2048], P('store', 'seq'), may hold values from -6 to 6
- draft_x: bfloat16 [192, 12288], P(None, 'store'), may hold values from -24 to 24
- w_query: bfloat16 [12288, 12288], P('store', 'seq'), may hold values from -0.0546875 to 0.0546875
- w_keyval: bfloat16 [12288, 2048], P('store'), may hold values from -0.0546875 to 0.0546875
Outputs:
- prefill_out: bfloat16 [32, 1024, 12288], P('store', None, 'seq')
- decode_out: bfloat16 [192, 12288], P('store', 'seq')
The draws below stay inside these ranges and needn't reach their ends.
Inputs may be any that keep to these rules, and one draw needn't show every extreme that they name: `page_home`: A permutation; slots s * 4 to s * 4 + 3 are held by store device s. `doc_page`: of the 24 entries of one group, at most 2 name pages held by one store device, and in every group some store device holds exactly 2 of them. Entries may repeat. `prefix_len`: some request has the full 512.
All inputs are finite; a program needn't handle non-finite values.
Results may differ from the reference program's by a relative error of at most 0.012.
The reference program's roundings to bfloat16 on the way count: a program that leaves them out, or rounds other values in their place, can miss the bound.
Values may be sent and summed in bfloat16 or wider, within the bound.
No kernel may reach another device: no remote copies, remote signals or barrier semaphores. Data moves between devices by JAX's collectives and lax.ppermute only.
A program may use at most 64 MiB of HBM per device.

```python
import jax
import jax.numpy as jnp
from jax import lax

D = 12288
QH = 96
KVH = 8
HD = 128
PAGE = 64
SUF = 1024
DRAFT = 3
SLOTS = 4
PAGES_REQ = 8
DEC_GRP = 2
GROUP = 12
PREF = 512
REQS = 3
NEED = 24
CAP = 2
GROUPS = 32
PAGES_ALL = 128
DEC_ROWS = 192


def shuffle_row(subkey, values_row):
    return jax.random.permutation(subkey, values_row)


def page_layout(key):
    perm_key, busy_key, pool_key, ranking_key, slot_key = jax.random.split(key, 5)
    slot_map = jax.random.permutation(perm_key, PAGES_ALL).astype(jnp.int32)
    busiest = jax.random.randint(busy_key, (GROUPS, 1), 0, GROUPS).astype(jnp.int32)
    holders = jnp.tile(jnp.arange(GROUPS, dtype=jnp.int32), CAP)
    holders = jnp.broadcast_to(holders[None, :], (GROUPS, GROUPS * CAP))
    shuffled = jax.vmap(shuffle_row)(jax.random.split(pool_key, GROUPS), holders)
    ranking = jnp.argsort((shuffled == busiest).astype(jnp.int32), axis=1, stable=True)
    others = jnp.take_along_axis(shuffled, ranking, axis=1)[:, :NEED - CAP]
    chosen = jnp.concatenate([jnp.broadcast_to(busiest, (GROUPS, CAP)), others], axis=1)
    blended = jax.vmap(shuffle_row)(jax.random.split(ranking_key, GROUPS), chosen)
    slot_pick = jax.random.randint(slot_key, (GROUPS, NEED), 0, SLOTS).astype(jnp.int32)
    physical = blended * SLOTS + slot_pick
    inverse = jnp.zeros((PAGES_ALL,), jnp.int32).at[slot_map].set(jnp.arange(PAGES_ALL, dtype=jnp.int32))
    logical = inverse[physical].reshape(GROUPS, REQS, PAGES_REQ)
    return (slot_map, logical)


def draw_page_home(key, part):
    return page_layout(key)[0]


def draw_doc_page(key, part):
    return page_layout(key)[1]


def draw_prefix_len(key, part):
    key = jax.random.fold_in(key, 3)
    length_key, pick_key = jax.random.split(key)
    lengths = jax.random.randint(length_key, (GROUPS, REQS), 1, PREF + 1).astype(jnp.int32)
    target = jax.random.randint(pick_key, (), 0, GROUPS * REQS)
    flat_index = jnp.arange(GROUPS * REQS).reshape(GROUPS, REQS)
    return jnp.where(flat_index == target, PREF, lengths).astype(jnp.int32)


def draw_suffix_q(key, part):
    key = jax.random.fold_in(key, 5)
    value_key = jax.random.fold_in(key, 0)
    values = jax.random.normal(value_key, (GROUPS, SUF, QH * HD), jnp.float32)
    return values.astype(jnp.bfloat16)


def draw_draft_x(key, part):
    key = jax.random.fold_in(key, 7)
    value_key = jax.random.fold_in(key, 0)
    values = 2.0 * jax.random.normal(value_key, (DEC_ROWS, D), jnp.float32)
    return values.astype(jnp.bfloat16)


def steps_of(stream_key, shape, shards, least, largest):
    loudness = 1.0
    for position, parts in shards:
        steps = jax.random.uniform(jax.random.fold_in(jax.random.fold_in(stream_key, 6), position), (parts,), jnp.float32, least / len(shards), largest / len(shards))
        loudness = loudness * jnp.repeat(jnp.exp(steps), shape[position] // parts).reshape((-1,) + (1,) * (len(shape) - 1 - position))
    return loudness


def centred(key, extent, width, reach, cuts=(), kind=jnp.bfloat16):
    result = width * jax.random.normal(key, extent, jnp.float32)
    if cuts:
        result = result * steps_of(key, extent, cuts, -0.22, 0.18)
    return jnp.clip(result, -reach, reach).astype(kind)


def setup_inputs(seed: int = 0) -> dict:
    splits = jax.random.split(jax.random.key(seed), 10)
    store_pages = centred(splits[0], (PAGES_ALL, PAGE, KVH * 2 * HD), 1.0, 6.0, ((0, 32),))
    page_home = draw_page_home(jax.random.fold_in(splits[9], 71), 0)
    doc_page = draw_doc_page(jax.random.fold_in(splits[9], 71), 0)
    prefix_len = draw_prefix_len(jax.random.fold_in(splits[9], 71), 0)
    suffix_q = draw_suffix_q(jax.random.fold_in(splits[9], 71), 0)
    suffix_kv = centred(splits[5], (GROUPS, SUF, KVH * 2 * HD), 1.0, 6.0, ((0, 32), (1, 16)))
    draft_x = draw_draft_x(jax.random.fold_in(splits[9], 71), 0)
    w_query = centred(splits[7], (D, QH * HD), D ** -0.5, 0.0546875, ((0, 32), (1, 16)))
    w_keyval = centred(splits[8], (D, KVH * 2 * HD), D ** -0.5, 0.0546875, ((0, 32),))
    return dict(store_pages=store_pages, page_home=page_home, doc_page=doc_page, prefix_len=prefix_len, suffix_q=suffix_q, suffix_kv=suffix_kv, draft_x=draft_x, w_query=w_query, w_keyval=w_keyval)


def attend(queries, far_keys, far_values, near_keys, near_values, live_mask, causal, score_scale):
    far_scores = jnp.dot(queries, far_keys.T, preferred_element_type=jnp.float32) * score_scale
    near_scores = jnp.dot(queries, near_keys.T, preferred_element_type=jnp.float32) * score_scale
    far_scores = jnp.where(live_mask, far_scores, -1e30)
    near_scores = jnp.where(causal, near_scores, -1e30)
    row_max = jnp.maximum(jnp.max(far_scores, axis=1), jnp.max(near_scores, axis=1))[:, None]
    far_weights = jnp.where(live_mask, jnp.exp(far_scores - row_max), 0.0)
    near_weights = jnp.where(causal, jnp.exp(near_scores - row_max), 0.0)
    row_total = jnp.sum(far_weights, axis=1) + jnp.sum(near_weights, axis=1)
    blended = jnp.dot(far_weights.astype(jnp.bfloat16), far_values, preferred_element_type=jnp.float32)
    blended = blended + jnp.dot(near_weights.astype(jnp.bfloat16), near_values, preferred_element_type=jnp.float32)
    return (blended / row_total[:, None]).astype(jnp.bfloat16)


def draft_attention(queries, prefix, drafts, lengths, score_scale):
    half_width = queries.shape[-1]
    query_wide = queries.astype(jnp.float32)
    far_scores = jnp.einsum('rtvhd,rpvd->rvthp', query_wide, prefix[..., :half_width].astype(jnp.float32)) * score_scale
    near_scores = jnp.einsum('rtvhd,rsvd->rvths', query_wide, drafts[..., :half_width].astype(jnp.float32)) * score_scale
    live_mask = (jnp.arange(prefix.shape[1])[None, :] < lengths[:, None])[:, None, None, None, :]
    draft_steps = drafts.shape[1]
    causal = (jnp.arange(draft_steps)[None, :] <= jnp.arange(draft_steps)[:, None])[None, None, :, None, :]
    far_scores = jnp.where(live_mask, far_scores, -1e30)
    near_scores = jnp.where(causal, near_scores, -1e30)
    row_max = jnp.maximum(jnp.max(far_scores, axis=4), jnp.max(near_scores, axis=4))[..., None]
    far_weights = jnp.where(live_mask, jnp.exp(far_scores - row_max), 0.0)
    near_weights = jnp.where(causal, jnp.exp(near_scores - row_max), 0.0)
    far_low = lax.optimization_barrier(far_weights.astype(jnp.bfloat16)).astype(jnp.float32)
    near_low = lax.optimization_barrier(near_weights.astype(jnp.bfloat16)).astype(jnp.float32)
    blended = jnp.einsum('rvthp,rpvd->rtvhd', far_low, prefix[..., half_width:].astype(jnp.float32))
    blended = blended + jnp.einsum('rvths,rsvd->rtvhd', near_low, drafts[..., half_width:].astype(jnp.float32))
    row_total = jnp.transpose(jnp.sum(far_weights, axis=4) + jnp.sum(near_weights, axis=4), (0, 2, 1, 3))
    return (blended / row_total[..., None]).astype(jnp.bfloat16)


def reference(store_pages, page_home, doc_page, prefix_len, suffix_q, suffix_kv, draft_x, w_query, w_keyval):
    score_scale = HD ** -0.5
    draft_query = jnp.dot(draft_x, w_query, preferred_element_type=jnp.float32).astype(jnp.bfloat16)
    draft_pairs = jnp.dot(draft_x, w_keyval, preferred_element_type=jnp.float32).astype(jnp.bfloat16)
    draft_query = draft_query.reshape(GROUPS, DEC_GRP, DRAFT, KVH, GROUP, HD)
    draft_pairs = draft_pairs.reshape(GROUPS, DEC_GRP, DRAFT, KVH, 2 * HD)
    causal = jnp.arange(SUF)[None, :] <= jnp.arange(SUF)[:, None]

    def one_group(group_index):
        slot_rows = page_home[doc_page[group_index]]
        prefix = store_pages[slot_rows].reshape(REQS, PREF, KVH, 2 * HD)
        lengths = prefix_len[group_index]
        queries = suffix_q[group_index].reshape(SUF, QH, HD)
        suffix = suffix_kv[group_index].reshape(SUF, KVH, 2 * HD)
        live_mask = jnp.arange(PREF)[None, :] < lengths[0]

        def one_head(head_index):
            kv_index = head_index // GROUP
            far_pairs = prefix[0, :, kv_index]
            near_pairs = suffix[:, kv_index]
            query_rows = queries[:, head_index]
            return attend(query_rows, far_pairs[:, :HD], far_pairs[:, HD:], near_pairs[:, :HD], near_pairs[:, HD:], live_mask, causal, score_scale)

        head_outputs = lax.map(one_head, jnp.arange(QH, dtype=jnp.int32))
        prefill_rows = jnp.transpose(head_outputs, (1, 0, 2)).reshape(SUF, QH * HD)
        decoded = draft_attention(draft_query[group_index], prefix[1:], draft_pairs[group_index], lengths[1:], score_scale)
        return prefill_rows, decoded.reshape(DEC_GRP * DRAFT, QH * HD)

    prefill_out, decode_out = lax.map(one_group, jnp.arange(GROUPS, dtype=jnp.int32))
    return prefill_out, decode_out.reshape(DEC_ROWS, QH * HD)
```

```python
import functools

import jax
import jax.numpy as jnp
from jax import lax
from jax.experimental import pallas as pl
from jax.experimental.pallas import tpu as pltpu
from jax.sharding import PartitionSpec as P

QH = 96
KVH = 8
HD = 128
X = 4
Y = 8
SEQ = 16
HEADS = 6
PAGE = 64
SLOTS = 4
NEED = 24
PREF = 512
SUF = 1024
ROWS = SUF // SEQ
DEC = 6
COLS = HEADS * HD + HD
BLOCKS = COLS // HD
PAGE_ROWS = SLOTS * PAGE
PART = X * DEC
SEND_Y = PAGE_ROWS + BLOCKS * 2 * PART
PICKS = 2 * Y
SEND_X = PICKS * PAGE + BLOCKS * 16
FETCH = NEED * PAGE
SWAP = FETCH + 16
SCALE = HD ** (-0.5)
EXP2 = SCALE * 1.4426950408889634
F32 = jnp.float32
BF16 = jnp.bfloat16
SMEM = pl.BlockSpec(memory_space=pltpu.SMEM)
VMEM = pl.BlockSpec(memory_space=pltpu.VMEM)


def params(mib):
    return pltpu.CompilerParams(vmem_limit_bytes=mib * 1024 * 1024)


def dot(a, b):
    return jnp.dot(a, b, preferred_element_type=F32)


def dot_t(a, b):
    return lax.dot_general(a, b, (((1,), (1,)), ((), ())), preferred_element_type=F32)


def split(values):
    high = values.astype(BF16).astype(F32)
    return jnp.concatenate([high, values - high], axis=0).astype(BF16)


def pack_kernel(q_ref, kv_ref, out_ref):
    out_ref[0, :, : HEADS * HD] = q_ref[...]
    out_ref[0, :, HEADS * HD :] = kv_ref[...]


def pack(queries, pairs):
    return pl.pallas_call(
        pack_kernel,
        grid=(SEQ,),
        in_specs=[
            pl.BlockSpec((ROWS, HEADS * HD), lambda i: (0, i)),
            pl.BlockSpec((ROWS, HD), lambda i: (0, i)),
        ],
        out_specs=pl.BlockSpec((1, ROWS, COLS), lambda i: (i, 0, 0)),
        out_shape=jax.ShapeDtypeStruct((SEQ, ROWS, COLS), BF16),
        compiler_params=params(16),
    )(queries, pairs)


def project_kernel(place, x_ref, wq_ref, wkv_ref, pages_ref, *outs):
    my_y = place[1]
    rows = Y * PART
    row = lax.broadcasted_iota(jnp.int32, (rows, rows), 0)
    col = lax.broadcasted_iota(jnp.int32, (rows, rows), 1)
    step, inner = row // PART, row % PART
    to_x, item = inner // DEC, inner % DEC
    to_y = (my_y + step) % Y
    pick = (col == (to_x * Y + to_y) * DEC + item).astype(F32).astype(BF16)
    ordered = dot(pick, x_ref[...]).astype(BF16)
    terms = [dot(ordered, wq_ref[...]), dot(ordered, wkv_ref[...])]
    pages = pages_ref[...].reshape(PAGE_ROWS, HD)
    for k in range(Y):
        outs[k][:PAGE_ROWS, :] = pages
        for n in range(BLOCKS):
            term = terms[0][:, n * HD : (n + 1) * HD] if n < HEADS else terms[1]
            base = PAGE_ROWS + n * 2 * PART
            outs[k][base : base + 2 * PART, :] = split(term[k * PART : (k + 1) * PART])


def project(place, x, w_query, w_keyval, store_pages):
    width = x.shape[1]
    return pl.pallas_call(
        project_kernel,
        grid_spec=pltpu.PrefetchScalarGridSpec(
            num_scalar_prefetch=1,
            grid=(1,),
            in_specs=[
                pl.BlockSpec((Y * PART, width), lambda i, p: (0, 0)),
                pl.BlockSpec((width, HEADS * HD), lambda i, p: (0, 0)),
                pl.BlockSpec((width, HD), lambda i, p: (0, p[2])),
                pl.BlockSpec((SLOTS, PAGE, HD), lambda i, p: (0, 0, p[2])),
            ],
            out_specs=[pl.BlockSpec((SEND_Y, HD), lambda i, p: (0, 0))] * Y,
        ),
        out_shape=[jax.ShapeDtypeStruct((SEND_Y, HD), BF16)] * Y,
        compiler_params=params(24),
    )(place, x, w_query, w_keyval, store_pages)


def route_kernel(place, doc, home, *refs):
    got, outs = refs[:Y], refs[Y : Y + X]
    pages, picks, seen = refs[Y + X :]
    my_x, my_y = place[0], place[1]
    for k in range(Y):
        pages[k * PAGE_ROWS : (k + 1) * PAGE_ROWS, :] = got[k][:PAGE_ROWS, :]

    def clear(i, carry):
        picks[i] = 0
        seen[2 * i] = 0
        seen[2 * i + 1] = 0
        return carry

    lax.fori_loop(0, X * PICKS, clear, 0)

    def note(i, carry):
        k = i // NEED
        group = ((my_x + k) % X) * Y + my_y
        place_in = home[doc[group * NEED + i - k * NEED]]
        holder = place_in // SLOTS
        rank = seen[k * X * Y + holder]
        seen[k * X * Y + holder] = rank + 1
        holder_y = holder % Y

        @pl.when(holder // Y == my_x)
        def _():
            spot = k * PICKS + holder_y * 2 + jnp.minimum(rank, 1)
            picks[spot] = ((my_y + Y - holder_y) % Y) * SLOTS + place_in % SLOTS

        return carry

    lax.fori_loop(0, X * NEED, note, 0)
    for k in range(X):
        for i in range(PICKS):
            start = pl.multiple_of(picks[k * PICKS + i] * PAGE, PAGE)
            outs[k][i * PAGE : (i + 1) * PAGE, :] = pages[pl.ds(start, PAGE), :]
    row = lax.broadcasted_iota(jnp.int32, (16, 2 * PART), 0)
    col = lax.broadcasted_iota(jnp.int32, (16, 2 * PART), 1)
    wanted = [
        (
            (row % 8 < DEC) & (col == (row // 8) * PART + ((my_x + k) % X) * DEC + row % 8)
        ).astype(F32).astype(BF16)
        for k in range(X)
    ]
    for n in range(BLOCKS):
        base = PAGE_ROWS + n * 2 * PART
        total = jnp.zeros((2 * PART, HD), F32)
        for k in range(Y):
            total = total + got[k][base : base + 2 * PART, :].astype(F32)
        both = split(total[:PART] + total[PART:])
        for k in range(X):
            spot = PICKS * PAGE + n * 16
            outs[k][spot : spot + 16, :] = dot(wanted[k], both).astype(BF16)


def route(place, doc, home, got):
    return pl.pallas_call(
        route_kernel,
        in_specs=[SMEM] * 3 + [VMEM] * Y,
        out_specs=[VMEM] * X,
        out_shape=[jax.ShapeDtypeStruct((SEND_X, HD), BF16)] * X,
        scratch_shapes=[
            pltpu.VMEM((Y * PAGE_ROWS, HD), BF16),
            pltpu.SMEM((X * PICKS,), jnp.int32),
            pltpu.SMEM((X * X * Y,), jnp.int32),
        ],
        compiler_params=params(16),
    )(place, doc, home, *got)


def collect_kernel(place, doc, home, *refs):
    got, (out_ref, q_ref), (seen,) = refs[:X], refs[X : X + 2], refs[X + 2 :]
    my_x, my_y = place[0], place[1]
    group = my_x * Y + my_y

    def clear(i, carry):
        seen[i] = 0
        return carry

    lax.fori_loop(0, X * Y, clear, 0)

    def note(i, carry):
        holder = home[doc[group * NEED + i]] // SLOTS
        rank = seen[holder]
        seen[holder] = rank + 1
        spot = (holder % Y) * 2 + jnp.minimum(rank, 1)
        start = pl.multiple_of(spot * PAGE, PAGE)
        far = (my_x + X - holder // Y) % X
        target = pl.ds(pl.multiple_of(i * PAGE, PAGE), PAGE)
        for k in range(X):

            @pl.when(far == k)
            def _():
                out_ref[target, :] = got[k][pl.ds(start, PAGE), :]

        return carry

    lax.fori_loop(0, NEED, note, 0)
    blank = jnp.zeros((8, HD), F32)
    for n in range(BLOCKS):
        spot = PICKS * PAGE + n * 16
        total = jnp.zeros((16, HD), F32)
        for k in range(X):
            total = total + got[k][spot : spot + 16, :].astype(F32)
        value = jnp.concatenate([total[:8] + total[8:], blank], axis=0).astype(BF16)
        if n < HEADS:
            q_ref[:, n * HD : (n + 1) * HD] = value
        else:
            out_ref[FETCH:, :] = value


def collect(place, doc, home, got):
    return pl.pallas_call(
        collect_kernel,
        in_specs=[SMEM] * 3 + [VMEM] * X,
        out_specs=[VMEM] * 2,
        out_shape=[
            jax.ShapeDtypeStruct((SWAP, HD), BF16),
            jax.ShapeDtypeStruct((16, HEADS * HD), BF16),
        ],
        scratch_shapes=[pltpu.SMEM((X * Y,), jnp.int32)],
        compiler_params=params(16),
    )(place, doc, home, *got)


def decode_kernel(place, lens, mine, other, q_ref, out_ref, keys, values):
    @pl.when(place[3] == 0)
    def _():
        keys[...] = mine[PREF:, :]
        values[...] = other[PREF:, :]

    @pl.when(place[3] == 1)
    def _():
        keys[...] = other[PREF:, :]
        values[...] = mine[PREF:, :]

    rows = HEADS * 8
    queries = jnp.concatenate(
        [q_ref[:, h * HD : (h + 1) * HD].astype(F32)[:8] for h in range(HEADS)], axis=0
    ).astype(BF16)
    half = DEC // 2
    item = lax.broadcasted_iota(jnp.int32, (rows, PREF), 0) % 8
    spot = lax.broadcasted_iota(jnp.int32, (rows, PREF), 1)
    scores, live = [], []
    for d in range(2):
        raw = dot_t(queries, keys[d * PREF : (d + 1) * PREF, :]) * SCALE
        ok = (item // half == d) & (spot < lens[d + 1])
        live.append(ok)
        scores.append(jnp.where(ok, raw, -1e30))
    near = dot_t(queries, keys[2 * PREF :, :]) * SCALE
    row = lax.broadcasted_iota(jnp.int32, near.shape, 0) % 8
    col = lax.broadcasted_iota(jnp.int32, near.shape, 1)
    near_ok = (col <= row) & (col // half == row // half) & (col < DEC)
    near = jnp.where(near_ok, near, -1e30)
    top = jnp.max(near, axis=1, keepdims=True)
    for part in scores:
        top = jnp.maximum(top, jnp.max(part, axis=1, keepdims=True))
    weight = jnp.where(near_ok, jnp.exp(near - top), 0.0)
    total = jnp.sum(weight, axis=1, keepdims=True)
    blend = dot(weight.astype(BF16), values[2 * PREF :, :])
    for d in range(2):
        weight = jnp.where(live[d], jnp.exp(scores[d] - top), 0.0)
        total = total + jnp.sum(weight, axis=1, keepdims=True)
        blend = blend + dot(weight.astype(BF16), values[d * PREF : (d + 1) * PREF, :])
    blend = blend / total
    for h in range(HEADS):
        out_ref[:, h * HD : (h + 1) * HD] = blend[h * 8 : h * 8 + DEC].astype(BF16)


def decode(place, lens, mine, other, queries):
    return pl.pallas_call(
        decode_kernel,
        in_specs=[SMEM] * 2 + [VMEM] * 3,
        out_specs=VMEM,
        out_shape=jax.ShapeDtypeStruct((DEC, HEADS * HD), BF16),
        scratch_shapes=[pltpu.VMEM((SWAP - PREF, HD), BF16)] * 2,
        compiler_params=params(16),
    )(place, lens, mine, other, queries)


TILE = 256


def prefill_kernel(place, lens, far_mine, far_other, near_mine, near_other, q_ref, out_ref, keys, values):
    @pl.when(pl.program_id(0) == 0)
    def _():
        def fill(far_keys, far_values, near_keys, near_values):
            alive = lax.broadcasted_iota(jnp.int32, (PREF, HD), 0) < lens[0]
            held = far_keys[:PREF, :].astype(F32)
            keys[:PREF, :] = jnp.where(alive, held, held[0:1]).astype(BF16)
            keys[PREF:, :] = near_keys[...]
            held = far_values[:PREF, :].astype(F32)
            values[:PREF, :HD] = jnp.where(alive, held, 0.0).astype(BF16)
            values[PREF:, :HD] = near_values[...]
            values[:PREF, HD:] = jnp.where(alive, 1.0, 0.0).astype(BF16)
            values[PREF:, HD:] = jnp.ones((SUF, HD), BF16)

        @pl.when(place[3] == 0)
        def _():
            fill(far_mine, far_other, near_mine, near_other)

        @pl.when(place[3] == 1)
        def _():
            fill(far_other, far_mine, near_other, near_mine)

    row = lax.broadcasted_iota(jnp.int32, (TILE, TILE), 0)
    col = lax.broadcasted_iota(jnp.int32, (TILE, TILE), 1)
    for i in range(SUF // TILE):
        done = PREF + i * TILE
        queries = q_ref[i * TILE : (i + 1) * TILE, :]
        full = dot_t(queries, keys[:done, :])
        edge = dot_t(queries, keys[done : done + TILE, :])
        edge = jnp.where(col <= row, edge, -1e30)
        top = jnp.maximum(
            jnp.max(full, axis=1, keepdims=True), jnp.max(edge, axis=1, keepdims=True)
        )
        blend = dot(jnp.exp2((full - top) * EXP2).astype(BF16), values[:done, :])
        blend = blend + dot(
            jnp.exp2((edge - top) * EXP2).astype(BF16), values[done : done + TILE, :]
        )
        out_ref[i * TILE : (i + 1) * TILE, :] = (blend[:, :HD] / blend[:, HD:]).astype(BF16)


def prefill(place, lens, far_mine, far_other, near_mine, near_other, queries):
    whole = lambda a: pl.BlockSpec(a.shape, lambda h: (0, 0))
    return pl.pallas_call(
        prefill_kernel,
        grid=(HEADS,),
        in_specs=[
            SMEM,
            SMEM,
            pl.BlockSpec((PREF, HD), lambda h: (0, 0)),
            pl.BlockSpec((PREF, HD), lambda h: (0, 0)),
            whole(near_mine),
            whole(near_other),
            pl.BlockSpec((SUF, HD), lambda h: (0, h)),
        ],
        out_specs=pl.BlockSpec((SUF, HD), lambda h: (0, h)),
        out_shape=jax.ShapeDtypeStruct((SUF, HEADS * HD), BF16),
        scratch_shapes=[
            pltpu.VMEM((PREF + SUF, HD), BF16),
            pltpu.VMEM((PREF + SUF, 2 * HD), BF16),
        ],
        compiler_params=params(40),
    )(place, lens, far_mine, far_other, near_mine, near_other, queries)


def local(
    store_pages, page_home, doc_page, prefix_len, suffix_q, suffix_kv, draft_x, w_query, w_keyval
):
    store_index = lax.axis_index("store")
    member = lax.axis_index("seq")
    place = jnp.stack([store_index // Y, store_index % Y, member, member % 2]).astype(jnp.int32)
    lens = lax.dynamic_index_in_dim(prefix_len, store_index, 0, keepdims=False)
    doc = doc_page.reshape(-1)
    along_y = lambda k: [(x * Y + y, x * Y + (y + k) % Y) for x in range(X) for y in range(Y)]
    along_x = lambda k: [(x * Y + y, (x + k) % X * Y + y) for x in range(X) for y in range(Y)]
    twins = [(i, i ^ 1) for i in range(SEQ)]

    packed = pack(suffix_q.reshape(ROWS, -1), suffix_kv.reshape(ROWS, -1))
    turned = lax.all_to_all(packed, "seq", split_axis=0, concat_axis=0, tiled=True)
    turned = turned.reshape(SUF, COLS)

    sent = project(place, draft_x, w_query, w_keyval, store_pages)
    got = [sent[0]] + [lax.ppermute(sent[k], "store", along_y(k)) for k in range(1, Y)]
    sent = route(place, doc, page_home, got)
    got = [sent[0]] + [lax.ppermute(sent[k], "store", along_x(k)) for k in range(1, X)]
    far_mine, draft_query = collect(place, doc, page_home, got)
    far_other = lax.ppermute(far_mine, "seq", twins)
    decoded = decode(place, lens, far_mine, far_other, draft_query)

    near_mine = turned[:, HEADS * HD :]
    near_other = lax.ppermute(near_mine, "seq", twins)
    prefilled = prefill(place, lens, far_mine, far_other, near_mine, near_other, turned)
    return prefilled.reshape(1, SUF, HEADS * HD), decoded


def solution(mesh):
    in_specs = (
        P("store", None, None),
        P(),
        P(),
        P(),
        P("store", "seq", None),
        P("store", "seq", None),
        P(None, "store"),
        P("store", "seq"),
        P("store", None),
    )
    out_specs = (P("store", None, "seq"), P("store", "seq"))
    return jax.shard_map(local, mesh=mesh, in_specs=in_specs, out_specs=out_specs, check_vma=False)
```
